32 devices in a mesh: grp: 2 (over x), cell: 16 (over z, y, core).
Axes of the slice: x: 2, y: 2, z: 4, core: 2. Of those that a mesh axis runs over, the one named last changes fastest.
Arguments:
- fields: bfloat16 [8192, 3, 8192], P(('grp', 'cell')), parts along dimension 0, may hold values from -6 to 6
- horiz: float32 [16384], P(('grp', 'cell')), parts along dimension 0, may hold values from 0.2 to 1
- vertical: float32 [16384], P(('grp', 'cell')), parts along dimension 0, may hold values from 1.5 to 6
- tilt_angle: float32 [16384], P(('grp', 'cell')), parts along dimension 0, may hold values from 0.2 to 1.4
- azimuth: float32 [16384], P(('grp', 'cell')), parts along dimension 0, may hold values from -3.140625 to 3.140625
- electrode_quads: int32 [4096, 4], P('grp'), parts along dimension 0, may hold values from 0 to 4095, as said below
Outputs:
- jacobian: bfloat16 [4096, 4, 8192], P('grp', None, 'cell'), parts along dimension 0
- coverage: float32 [16384], P(('grp', 'cell')), parts along dimension 0
The draws below stay inside these ranges and needn't reach their ends.
There are 2 independent parts, one for each index of `grp`. The reference program is written for one: setup_inputs(seed, part) draws one part's arguments, and reference() takes and returns one part's arrays. A program takes and returns all parts, laid end to end along the dimension named above; each array names one. Nothing has to cross between parts.
Inputs may be any that keep to these rules, and one draw needn't show every extreme that they name: `electrode_quads`: each row names four different electrodes.
All inputs are finite; a program needn't handle non-finite values.
Results may differ from the reference program's by a relative error of at most 0.001.
Values may be sent and summed in bfloat16 or wider, within the bound.
A program may use at most 192 MiB of HBM per device.

```python
import math
import jax
import jax.numpy as jnp
from jax import lax

ELECTRODE_COUNT = 4096
QUAD_READINGS = 2048
CELL_TOTAL = 8192


def draw_electrode_quads(key, part):
    random_keys = jax.random.split(key, 4)
    base_offset = jax.random.randint(random_keys[0], (QUAD_READINGS,), 0, ELECTRODE_COUNT)
    base_offset = base_offset.at[0].set(ELECTRODE_COUNT - 1).at[1].set(0)
    quarter_size = ELECTRODE_COUNT // 4
    first_quarter = jax.random.randint(random_keys[1], (QUAD_READINGS,), 1, quarter_size)
    second_quarter = jax.random.randint(random_keys[2], (QUAD_READINGS,), quarter_size, 2 * quarter_size)
    third_quarter = jax.random.randint(random_keys[3], (QUAD_READINGS,), 2 * quarter_size, 3 * quarter_size)
    return jnp.stack([base_offset, (base_offset + first_quarter) % ELECTRODE_COUNT, (base_offset + second_quarter) % ELECTRODE_COUNT, (base_offset + third_quarter) % ELECTRODE_COUNT], axis=1).astype(jnp.int32)


def block_scale(own_key, dims, cuts, low, top_value):
    def one(dim, blocks):
        steps = jax.random.uniform(jax.random.fold_in(jax.random.fold_in(own_key, 6), dim), (blocks,), jnp.float32, low / len(cuts), top_value / len(cuts))
        return jnp.repeat(jnp.exp(steps), dims[dim] // blocks).reshape((-1,) + (1,) * (len(dims) - dim - 1))

    level = one(*cuts[0])
    for cut in cuts[1:]:
        level = level * one(*cut)
    return level


def gaussian(rng, extent, width, most, cuts=(), held_as=jnp.bfloat16):
    drawn = width * jax.random.normal(rng, extent, jnp.float32)
    if cuts:
        drawn = drawn * block_scale(rng, extent, cuts, -0.22, 0.18)
    return jnp.clip(drawn, -most, most).astype(held_as)


def setup_inputs(seed: int = 0, part: int = 0) -> dict:
    streams_of = jax.random.split(jax.random.key(seed), 7)
    part_keys = jax.random.split(jax.random.fold_in(streams_of[6], part), 7)
    fields = gaussian(part_keys[0], (ELECTRODE_COUNT, 3, CELL_TOTAL), 1.0, 6.0, ((0, 16),))
    horiz = jnp.clip(jnp.exp(math.log(1.0) - 1.609438 * jax.random.uniform(part_keys[1], (CELL_TOTAL,), jnp.float32) ** block_scale(part_keys[1], (CELL_TOTAL,), ((0, 16),), -0.2, 0.2)), 0.2, 1.0)
    vertical = jnp.clip(jnp.exp(math.log(6.0) - 1.3862944 * jax.random.uniform(part_keys[2], (CELL_TOTAL,), jnp.float32) ** block_scale(part_keys[2], (CELL_TOTAL,), ((0, 16),), -0.2, 0.2)), 1.5, 6.0)
    tilt_angle = jnp.clip(0.2 + 1.19999997 * jax.random.uniform(part_keys[3], (CELL_TOTAL,), jnp.float32) ** block_scale(part_keys[3], (CELL_TOTAL,), ((0, 16),), -0.2, 0.2), 0.2, 1.4)
    azimuth = jnp.clip(jax.random.uniform(part_keys[4], (CELL_TOTAL,), jnp.float32, -3.140625, 3.140625), -3.140625, 3.140625)
    electrode_quads = draw_electrode_quads(jax.random.fold_in(jax.random.fold_in(streams_of[6], part), 71), part)
    return {"fields": fields, "horiz": horiz, "vertical": vertical, "tilt_angle": tilt_angle, "azimuth": azimuth, "electrode_quads": electrode_quads}


def sensitivity(grads, horiz, vertical, tilt_angle, azimuth, rows):

    def pick(column):
        return jnp.take(grads, rows[:, column], axis=0).astype(jnp.float32)
    source = pick(0) - pick(1)
    receiver = pick(2) - pick(3)
    sin_t = jnp.sin(tilt_angle)
    cos_t = jnp.cos(tilt_angle)
    sin_p = jnp.sin(azimuth)
    cos_p = jnp.cos(azimuth)
    axis_dir = jnp.stack([sin_t * cos_p, sin_t * sin_p, cos_t])
    tilt_dir = jnp.stack([cos_t * cos_p, cos_t * sin_p, -sin_t])
    turn_dir = jnp.stack([-sin_t * sin_p, sin_t * cos_p, jnp.zeros_like(sin_t)])

    def along(field, direction):
        return lax.optimization_barrier(jnp.sum(field * direction[None], axis=1))
    s_axis = along(source, axis_dir)
    r_axis = along(receiver, axis_dir)
    s_tilt = along(source, tilt_dir)
    r_tilt = along(receiver, tilt_dir)
    s_turn = along(source, turn_dir)
    r_turn = along(receiver, turn_dir)
    inner = lax.optimization_barrier(jnp.sum(source * receiver, axis=1))
    contrast = vertical - horiz
    return jnp.stack([-horiz * (inner - s_axis * r_axis), -vertical * s_axis * r_axis, -contrast * (s_tilt * r_axis + s_axis * r_tilt), -contrast * (s_turn * r_axis + s_axis * r_turn)], axis=1)

def reference(fields, horiz, vertical, tilt_angle, azimuth, electrode_quads):
    block_slice = min(128, QUAD_READINGS)
    block_count = QUAD_READINGS // block_slice

    def one_block(rows):
        values = sensitivity(fields, horiz, vertical, tilt_angle, azimuth, rows)
        meansq = lax.optimization_barrier(jnp.sum(values * values, axis=(1, 2))) / (4.0 * CELL_TOTAL)
        normed = values * lax.rsqrt(meansq + 1e-06)[:, None, None]
        return (normed.astype(jnp.bfloat16), lax.optimization_barrier(jnp.sum(normed * normed, axis=(0, 1))))
    jacobian_blocks, coverage_blocks = lax.map(one_block, electrode_quads.reshape(block_count, block_slice, 4))
    return (jacobian_blocks.reshape(QUAD_READINGS, 4, CELL_TOTAL), lax.optimization_barrier(jnp.sum(coverage_blocks, axis=0)))
```

```python
import functools

import jax
import jax.numpy as jnp
from jax import lax
from jax.experimental import pallas as pl
from jax.experimental.pallas import tpu as pltpu
from jax.sharding import PartitionSpec as P

MESH = pl.DeviceIdType.MESH
LANES = 128
DEPTH = 256
UNROLL = 16
TILE = 1024


def greet(n, me):
    barrier = pltpu.get_barrier_semaphore()

    @pl.loop(1, n)
    def _(step):
        pl.semaphore_signal(barrier, inc=1, device_id={"cell": lax.rem(me + step, n)}, device_id_type=MESH)

    pl.semaphore_wait(barrier, n - 1)


def fill_coefficients(coef, horiz, vertical, tilt_angle, azimuth):
    sin_t, cos_t = jnp.sin(tilt_angle), jnp.cos(tilt_angle)
    sin_p, cos_p = jnp.sin(azimuth), jnp.cos(azimuth)
    rows = (
        sin_t * cos_p, sin_t * sin_p, cos_t,
        cos_t * cos_p, cos_t * sin_p, -sin_t,
        -sin_t * sin_p, sin_t * cos_p,
        -horiz, -vertical, horiz - vertical,
    )
    for k, row in enumerate(rows):
        coef[k] = row


def spread_quads(quads, block_of, place_of):
    for k in range(4):
        @pl.loop(0, quads.shape[1] // LANES)
        def _(i):
            at = pl.multiple_of(i * LANES, LANES)
            row = quads[pl.ds(k, 1), pl.ds(at, LANES)]
            block = row // DEPTH
            for target, value in ((block_of, block), (place_of, row - block * DEPTH)):
                wide = jnp.broadcast_to(value.astype(jnp.float32), (LANES, LANES))
                target[k, pl.ds(at, LANES), :] = wide.T.astype(jnp.bfloat16)


def add_group(chunk, group, landed, block_of, place_of, diffs):
    readings = diffs.shape[1]
    lane = lax.broadcasted_iota(jnp.int32, (TILE, LANES), 1).astype(jnp.float32)
    lanes = [(lane + LANES * h).astype(jnp.bfloat16) for h in range(DEPTH // LANES)]
    here = jnp.full((TILE, LANES), group, jnp.int32).astype(jnp.float32).astype(jnp.bfloat16)
    one, none = jnp.bfloat16(1), jnp.bfloat16(0)
    away = jnp.bfloat16(-1)

    @pl.loop(0, readings // TILE)
    def _(t):
        at = pl.multiple_of(t * TILE, TILE)
        rows = pl.ds(pl.multiple_of(group * DEPTH, DEPTH), DEPTH)
        grads = jnp.concatenate([landed[chunk, c, rows, :] for c in range(3)], axis=-1)
        for pair in range(2):
            plus, minus = (
                jnp.where(block_of[k, pl.ds(at, TILE), :] == here, place_of[k, pl.ds(at, TILE), :], away)
                for k in (2 * pair, 2 * pair + 1)
            )
            select = jnp.concatenate(
                [jnp.where(plus == x, one, jnp.where(minus == x, -one, none)) for x in lanes], axis=-1
            )
            out = jnp.dot(select, grads, preferred_element_type=jnp.float32)
            for c in range(3):
                diffs[3 * pair + c, pl.ds(at, TILE), :] += out[:, c * LANES:(c + 1) * LANES]


def chunk_sensitivities(chunk, coef, diffs, sens, squares):
    readings = squares.shape[0]
    tile = 32

    @pl.loop(0, readings // tile)
    def _(i):
        at = pl.multiple_of(i * tile, tile)
        s = [diffs[c, pl.ds(at, tile), :] for c in range(3)]
        r = [diffs[3 + c, pl.ds(at, tile), :] for c in range(3)]
        k = [coef[j, pl.ds(chunk, 1), :] for j in range(11)]
        sn, rn = (f[0] * k[0] + f[1] * k[1] + f[2] * k[2] for f in (s, r))
        st, rt = (f[0] * k[3] + f[1] * k[4] + f[2] * k[5] for f in (s, r))
        sp, rp = (f[0] * k[6] + f[1] * k[7] for f in (s, r))
        dot = s[0] * r[0] + s[1] * r[1] + s[2] * r[2]
        both = sn * rn
        values = (
            k[8] * (dot - both), k[9] * both, k[10] * (st * rn + sn * rt), k[10] * (sp * rn + sn * rp)
        )
        square = squares[pl.ds(at, tile), :]
        for p, value in enumerate(values):
            sens[chunk, pl.ds(4 * at + p, tile, stride=4), :] = value
            square = square + value * value
        squares[pl.ds(at, tile), :] = square


def flip(a, b, n):
    out, weight = 0, 1
    while weight < n:
        out = out + (a // weight + b // weight) % 2 * weight
        weight *= 2
    return out


def exchange_kernel(
    n, quads_hbm, fields, horiz, vertical, tilt_angle, azimuth, sens, total,
    landed, diffs, squares, coef, cells_of, quads, block_of, place_of, part, slots,
    send_sem, recv_sem, own_sem, small_sem, part_send_sem, part_recv_sem,
):
    me = lax.axis_index("cell")
    rows = fields.shape[1]
    chunks = landed.shape[0]
    readings = squares.shape[0]
    cells = chunks * LANES
    groups = rows * n // DEPTH
    members = DEPTH // rows
    my_group = me // members
    paired = n & (n - 1) == 0
    greet(n, me)

    def landing(chunk):
        return landed.at[chunk, :, pl.ds(pl.multiple_of(me * rows, rows), rows), :]

    def leaving(device, chunk):
        return fields.at[:, :, pl.ds(pl.multiple_of(device * cells + chunk * LANES, LANES), LANES)]

    def copy(chunk, peer, source):
        return pltpu.make_async_remote_copy(
            src_ref=leaving(peer, chunk),
            dst_ref=landing(chunk),
            send_sem=send_sem.at[chunk, peer],
            recv_sem=recv_sem.at[chunk, source],
            device_id={"cell": peer},
            device_id_type=MESH,
        )

    def own(chunk):
        return pltpu.make_async_copy(leaving(me, chunk), landing(chunk), own_sem.at[chunk])

    def partner(chunk, step):
        around = lax.rem(me + step, n)
        if not paired:
            return around
        last = (chunk + 1) // chunks
        across = flip(me, step % 2 * (n // 2) + step // 2, n)
        return last * across + (1 - last) * around

    def turn_group(chunk, turn):
        around = lax.rem(my_group - turn + groups, groups)
        if not paired:
            return around
        last = (chunk + 1) // chunks
        return last * flip(my_group, turn, groups) + (1 - last) * around

    @pl.loop(0, chunks)
    def _(chunk):
        @pl.loop(1, n)
        def _(step):
            copy(chunk, partner(chunk, step), me).start()

        own(chunk).start()

    smalls = [pltpu.make_async_copy(quads_hbm, quads, small_sem.at[4])] + [
        pltpu.make_async_copy(x, cells_of.at[k], small_sem.at[k])
        for k, x in enumerate((horiz, vertical, tilt_angle, azimuth))
    ]
    for small in smalls:
        small.start()
    squares[...] = jnp.zeros_like(squares)
    for small in smalls:
        small.wait()
    fill_coefficients(coef, *(cells_of[k] for k in range(4)))
    spread_quads(quads, block_of, place_of)

    @pl.loop(0, chunks)
    def _(chunk):
        @pl.loop(0, readings // LANES)
        def _(i):
            at = pl.multiple_of(i * LANES, LANES)
            for c in range(6):
                diffs[c, pl.ds(at, LANES), :] = jnp.zeros((LANES, LANES), jnp.float32)

        @pl.loop(0, groups)
        def _(turn):
            group = turn_group(chunk, turn)

            @pl.loop(0, members)
            def _(k):
                source = group * members + k

                @pl.when(source == me)
                def _():
                    own(chunk).wait()

                @pl.when(source != me)
                def _():
                    copy(chunk, source, source).wait_recv()

            add_group(chunk, group, landed, block_of, place_of, diffs)

        chunk_sensitivities(chunk, coef, diffs, sens, squares)

    def copy_part(step):
        return pltpu.make_async_remote_copy(
            src_ref=part,
            dst_ref=slots.at[step],
            send_sem=part_send_sem.at[step],
            recv_sem=part_recv_sem.at[step],
            device_id={"cell": lax.rem(me + step, n)},
            device_id_type=MESH,
        )

    depth = readings // LANES
    lane = lax.broadcasted_iota(jnp.int32, (depth, LANES), 1)

    def gather_sum(j, packed):
        at = pl.multiple_of(j * depth, depth)
        return jnp.where(lane == j, jnp.sum(squares[pl.ds(at, depth), :], axis=-1, keepdims=True), packed)

    part[...] = lax.fori_loop(0, LANES, gather_sum, jnp.zeros((depth, LANES), jnp.float32), unroll=8)

    @pl.loop(1, n)
    def _(step):
        copy_part(step).start()

    slots[0] = part[...]

    @pl.loop(0, chunks)
    def _(chunk):
        @pl.loop(1, n)
        def _(step):
            copy(chunk, lax.rem(me + step, n), me).wait_send()

    @pl.loop(1, n)
    def _(step):
        copy_part(step).wait()

    total[...] = jnp.sum(slots[...], axis=0)


def sensitivities(fields, quads, cell_values, n):
    comps, rows, _ = fields.shape
    chunks = cell_values[0].shape[0]
    electrodes, readings = rows * n, quads.shape[1]
    sums = (readings // LANES, LANES)
    in_vmem = pl.BlockSpec(memory_space=pltpu.VMEM)
    anywhere = pl.BlockSpec(memory_space=pl.ANY)
    return pl.pallas_call(
        functools.partial(exchange_kernel, n),
        out_shape=[
            pltpu.VMEM((chunks, readings * 4, LANES), jnp.float32),
            jax.ShapeDtypeStruct(sums, jnp.float32),
        ],
        in_specs=[anywhere] * (2 + len(cell_values)),
        out_specs=[in_vmem, in_vmem],
        scratch_shapes=[
            pltpu.VMEM((chunks, comps, electrodes, LANES), fields.dtype),
            pltpu.VMEM((2 * comps, readings, LANES), jnp.float32),
            pltpu.VMEM((readings, LANES), jnp.float32),
            pltpu.VMEM((11, chunks, LANES), jnp.float32),
            pltpu.VMEM((4, chunks, LANES), jnp.float32),
            pltpu.VMEM(quads.shape, quads.dtype),
            pltpu.VMEM((4, readings, LANES), jnp.bfloat16),
            pltpu.VMEM((4, readings, LANES), jnp.bfloat16),
            pltpu.VMEM(sums, jnp.float32),
            pltpu.VMEM((n, *sums), jnp.float32),
            pltpu.SemaphoreType.DMA((chunks, n)),
            pltpu.SemaphoreType.DMA((chunks, n)),
            pltpu.SemaphoreType.DMA((chunks,)),
            pltpu.SemaphoreType.DMA((5,)),
            pltpu.SemaphoreType.DMA((n,)),
            pltpu.SemaphoreType.DMA((n,)),
        ],
        compiler_params=pltpu.CompilerParams(
            collective_id=0, has_side_effects=True, vmem_limit_bytes=40 * 2**20
        ),
        name="exchange",
    )(quads, fields, *cell_values)


def norm_kernel(count, sens, total, jacobian, coverage, scale):
    depth = total.shape[0]
    readings, _, cells = jacobian.shape
    step = pl.program_id(0)

    @pl.when(step == 0)
    def _():
        coverage[...] = jnp.zeros_like(coverage)
        value = lax.rsqrt(total[...] / count + 1e-06)
        for p in range(4):
            scale[pl.ds(p, depth, stride=4), :] = value

    wide = 4 * depth
    lane = lax.broadcasted_iota(jnp.int32, (wide, LANES), 1)

    first = step * (readings // depth)

    def some(g, sums):
        columns = [
            jnp.sum(jnp.where(lane == first + UNROLL * g + u, scale[...], 0.0), axis=-1, keepdims=True)
            for u in range(UNROLL)
        ]
        for u in range(UNROLL):
            i = UNROLL * g + u
            rows = pl.ds(pl.multiple_of((first + i) * wide, wide), wide)
            put = pl.ds(pl.multiple_of(i * depth, depth), depth)
            for c in range(cells // LANES):
                normed = sens[c, rows, :] * columns[u]
                jacobian[put, :, pl.ds(c * LANES, LANES)] = normed.reshape(depth, 4, LANES).astype(jnp.bfloat16)
                square = jnp.sum((normed * normed).reshape(wide // 8, 8, LANES), axis=0)
                sums = sums[:c] + (sums[c] + square,) + sums[c + 1:]
        return sums

    sums = lax.fori_loop(
        0, readings // depth // UNROLL, some,
        tuple(coverage[:, pl.ds(c * LANES, LANES)] for c in range(cells // LANES)),
    )
    for c, total_of in enumerate(sums):
        coverage[:, pl.ds(c * LANES, LANES)] = total_of


def normalise(sens, total, count):
    chunks, rows, _ = sens.shape
    readings, cells = rows // 4, chunks * LANES
    block = 512
    return pl.pallas_call(
        functools.partial(norm_kernel, count),
        grid=(readings // block,),
        in_specs=[
            pl.BlockSpec(memory_space=pltpu.VMEM),
            pl.BlockSpec(memory_space=pltpu.VMEM),
        ],
        out_specs=[
            pl.BlockSpec((block, 4, cells), lambda i: (i, 0, 0)),
            pl.BlockSpec((8, cells), lambda i: (0, 0)),
        ],
        out_shape=[
            jax.ShapeDtypeStruct((readings, 4, cells), jnp.bfloat16),
            jax.ShapeDtypeStruct((8, cells), jnp.float32),
        ],
        scratch_shapes=[pltpu.VMEM((4 * total.shape[0], LANES), jnp.float32)],
        compiler_params=pltpu.CompilerParams(vmem_limit_bytes=8 * 2**20),
        name="norm",
    )(pltpu.with_memory_space_constraint(sens, pltpu.VMEM), total)


def local(fields, horiz, vertical, tilt_angle, azimuth, electrode_quads):
    shards = lax.axis_size("cell")
    cells = horiz.shape[0]
    sens, total = sensitivities(
        fields.transpose(1, 0, 2),
        electrode_quads.T,
        [x.reshape(cells // LANES, LANES) for x in (horiz, vertical, tilt_angle, azimuth)],
        shards,
    )
    jacobian, coverage = normalise(sens, total, 4.0 * cells * shards)
    return jacobian, jnp.sum(coverage, axis=0)


def solution(mesh):
    placed = (
        P(("grp", "cell"), None, None),
        P(("grp", "cell")),
        P(("grp", "cell")),
        P(("grp", "cell")),
        P(("grp", "cell")),
        P("grp", None),
    )
    return jax.shard_map(
        local,
        mesh=mesh,
        in_specs=placed,
        out_specs=(P("grp", None, "cell"), P(("grp", "cell"))),
        check_vma=False,
    )
```

```python
import functools

import jax
import jax.numpy as jnp
from jax import lax
from jax.experimental import pallas as pl
from jax.experimental.pallas import tpu as pltpu
from jax.sharding import PartitionSpec as P

MESH = pl.DeviceIdType.MESH
LANES = 128
DEPTH = 256
UNROLL = 16
TILE = 1024


def greet(n, me):
    barrier = pltpu.get_barrier_semaphore()

    @pl.loop(1, n)
    def _(step):
        pl.semaphore_signal(barrier, inc=1, device_id={"cell": lax.rem(me + step, n)}, device_id_type=MESH)

    pl.semaphore_wait(barrier, n - 1)


def fill_coefficients(coef, horiz, vertical, tilt_angle, azimuth):
    sin_t, cos_t = jnp.sin(tilt_angle), jnp.cos(tilt_angle)
    sin_p, cos_p = jnp.sin(azimuth), jnp.cos(azimuth)
    rows = (
        sin_t * cos_p, sin_t * sin_p, cos_t,
        cos_t * cos_p, cos_t * sin_p, -sin_t,
        -sin_t * sin_p, sin_t * cos_p,
        -horiz, -vertical, horiz - vertical,
    )
    for k, row in enumerate(rows):
        coef[k] = row


def spread_quads(quads, block_of, place_of):
    for k in range(4):
        @pl.loop(0, quads.shape[1] // LANES)
        def _(i):
            at = pl.multiple_of(i * LANES, LANES)
            row = quads[pl.ds(k, 1), pl.ds(at, LANES)]
            block = row // DEPTH
            for target, value in ((block_of, block), (place_of, row - block * DEPTH)):
                wide = jnp.broadcast_to(value.astype(jnp.float32), (LANES, LANES))
                target[k, pl.ds(at, LANES), :] = wide.T.astype(jnp.bfloat16)


def add_group(chunk, group, landed, block_of, place_of, diffs):
    readings = diffs.shape[2]
    lane = lax.broadcasted_iota(jnp.int32, (TILE, LANES), 1).astype(jnp.float32)
    lanes = [(lane + LANES * h).astype(jnp.bfloat16) for h in range(DEPTH // LANES)]
    here = jnp.full((TILE, LANES), group, jnp.int32).astype(jnp.float32).astype(jnp.bfloat16)
    one, none = jnp.bfloat16(1), jnp.bfloat16(0)
    away = jnp.bfloat16(-1)

    @pl.loop(0, readings // TILE)
    def _(t):
        at = pl.multiple_of(t * TILE, TILE)
        rows = pl.ds(pl.multiple_of(group * DEPTH, DEPTH), DEPTH)
        grads = jnp.concatenate([landed[chunk, c, rows, :] for c in range(3)], axis=-1)
        for pair in range(2):
            plus, minus = (
                jnp.where(block_of[k, pl.ds(at, TILE), :] == here, place_of[k, pl.ds(at, TILE), :], away)
                for k in (2 * pair, 2 * pair + 1)
            )
            select = jnp.concatenate(
                [jnp.where(plus == x, one, jnp.where(minus == x, -one, none)) for x in lanes], axis=-1
            )
            out = jnp.dot(select, grads, preferred_element_type=jnp.float32)
            for c in range(3):
                diffs[chunk % 2, 3 * pair + c, pl.ds(at, TILE), :] += out[:, c * LANES:(c + 1) * LANES]


def chunk_sensitivities(chunk, coef, diffs, sens, squares):
    readings = squares.shape[0]
    tile = 32

    @pl.loop(0, readings // tile)
    def _(i):
        at = pl.multiple_of(i * tile, tile)
        s = [diffs[chunk % 2, c, pl.ds(at, tile), :] for c in range(3)]
        r = [diffs[chunk % 2, 3 + c, pl.ds(at, tile), :] for c in range(3)]
        k = [coef[j, pl.ds(chunk, 1), :] for j in range(11)]
        sn, rn = (f[0] * k[0] + f[1] * k[1] + f[2] * k[2] for f in (s, r))
        st, rt = (f[0] * k[3] + f[1] * k[4] + f[2] * k[5] for f in (s, r))
        sp, rp = (f[0] * k[6] + f[1] * k[7] for f in (s, r))
        dot = s[0] * r[0] + s[1] * r[1] + s[2] * r[2]
        both = sn * rn
        values = (
            k[8] * (dot - both), k[9] * both, k[10] * (st * rn + sn * rt), k[10] * (sp * rn + sn * rp)
        )
        square = squares[pl.ds(at, tile), :]
        for p, value in enumerate(values):
            sens[chunk, pl.ds(4 * at + p, tile, stride=4), :] = value
            square = square + value * value
        squares[pl.ds(at, tile), :] = square


def flip(a, b, n):
    out, weight = 0, 1
    while weight < n:
        out = out + (a // weight + b // weight) % 2 * weight
        weight *= 2
    return out


def exchange_kernel(
    n, quads_hbm, fields, horiz, vertical, tilt_angle, azimuth, sens, total,
    landed, diffs, squares, coef, cells_of, quads, block_of, place_of, part, slots,
    send_sem, recv_sem, own_sem, small_sem, part_send_sem, part_recv_sem,
):
    me = lax.axis_index("cell")
    rows = fields.shape[1]
    chunks = landed.shape[0]
    readings = squares.shape[0]
    cells = chunks * LANES
    groups = rows * n // DEPTH
    members = DEPTH // rows
    my_group = me // members
    paired = n & (n - 1) == 0
    greet(n, me)

    def landing(chunk):
        return landed.at[chunk, :, pl.ds(pl.multiple_of(me * rows, rows), rows), :]

    def leaving(device, chunk):
        return fields.at[:, :, pl.ds(pl.multiple_of(device * cells + chunk * LANES, LANES), LANES)]

    def copy(chunk, peer, source):
        return pltpu.make_async_remote_copy(
            src_ref=leaving(peer, chunk),
            dst_ref=landing(chunk),
            send_sem=send_sem.at[chunk, peer],
            recv_sem=recv_sem.at[chunk, source],
            device_id={"cell": peer},
            device_id_type=MESH,
        )

    def own(chunk):
        return pltpu.make_async_copy(leaving(me, chunk), landing(chunk), own_sem.at[chunk])

    def partner(chunk, step):
        around = lax.rem(me + step, n)
        if not paired:
            return around
        last = (chunk + 1) // chunks
        across = flip(me, step % 2 * (n // 2) + step // 2, n)
        return last * across + (1 - last) * around

    half = groups // 2
    upper = my_group // max(half, 1)

    def turn_group(chunk, turn):
        if not paired:
            return lax.rem(my_group - turn + groups, groups)
        across = flip(my_group, turn, groups)
        far = turn // half
        last = (chunk + 1) // chunks
        inward = upper * (turn - half) + (1 - upper) * (groups - 1 - (turn - half))
        direct = far * (1 - last)
        return direct * inward + (1 - direct) * across

    @pl.loop(0, chunks)
    def _(chunk):
        @pl.loop(1, n)
        def _(step):
            copy(chunk, partner(chunk, step), me).start()

        own(chunk).start()

    smalls = [pltpu.make_async_copy(quads_hbm, quads, small_sem.at[4])] + [
        pltpu.make_async_copy(x, cells_of.at[k], small_sem.at[k])
        for k, x in enumerate((horiz, vertical, tilt_angle, azimuth))
    ]
    for small in smalls:
        small.start()
    squares[...] = jnp.zeros_like(squares)
    for small in smalls:
        small.wait()
    fill_coefficients(coef, *(cells_of[k] for k in range(4)))
    spread_quads(quads, block_of, place_of)

    def take(chunk, first, count):
        @pl.loop(0, count)
        def _(turn):
            group = turn_group(chunk, first + turn)

            @pl.loop(0, members)
            def _(k):
                source = group * members + k

                @pl.when(source == me)
                def _():
                    own(chunk).wait()

                @pl.when(source != me)
                def _():
                    copy(chunk, source, source).wait_recv()

            add_group(chunk, group, landed, block_of, place_of, diffs)

    def take_near(chunk):
        @pl.loop(0, readings // LANES)
        def _(i):
            at = pl.multiple_of(i * LANES, LANES)
            for c in range(6):
                diffs[chunk % 2, c, pl.ds(at, LANES), :] = jnp.zeros((LANES, LANES), jnp.float32)

        take(chunk, 0, half)

    take_near(0)

    @pl.loop(0, chunks)
    def _(chunk):
        @pl.when(chunk + 1 < chunks)
        def _():
            take_near(chunk + 1)

        take(chunk, half, groups - half)
        chunk_sensitivities(chunk, coef, diffs, sens, squares)

    def copy_part(step):
        peer = flip(me, n - step, n) if paired else lax.rem(me + n - step, n)
        return pltpu.make_async_remote_copy(
            src_ref=part,
            dst_ref=slots.at[step],
            send_sem=part_send_sem.at[step],
            recv_sem=part_recv_sem.at[step],
            device_id={"cell": peer},
            device_id_type=MESH,
        )

    depth = readings // LANES
    lane = lax.broadcasted_iota(jnp.int32, (depth, LANES), 1)

    def gather_sum(j, packed):
        at = pl.multiple_of(j * depth, depth)
        return jnp.where(lane == j, jnp.sum(squares[pl.ds(at, depth), :], axis=-1, keepdims=True), packed)

    part[...] = lax.fori_loop(0, LANES, gather_sum, jnp.zeros((depth, LANES), jnp.float32), unroll=32)

    @pl.loop(1, n)
    def _(step):
        copy_part(step).start()

    slots[0] = part[...]

    @pl.loop(0, chunks)
    def _(chunk):
        @pl.loop(1, n)
        def _(step):
            copy(chunk, lax.rem(me + step, n), me).wait_send()

    @pl.loop(1, n)
    def _(step):
        copy_part(step).wait()

    total[...] = jnp.sum(slots[...], axis=0)


def sensitivities(fields, quads, cell_values, n):
    comps, rows, _ = fields.shape
    chunks = cell_values[0].shape[0]
    electrodes, readings = rows * n, quads.shape[1]
    sums = (readings // LANES, LANES)
    in_vmem = pl.BlockSpec(memory_space=pltpu.VMEM)
    anywhere = pl.BlockSpec(memory_space=pl.ANY)
    return pl.pallas_call(
        functools.partial(exchange_kernel, n),
        out_shape=[
            pltpu.VMEM((chunks, readings * 4, LANES), jnp.float32),
            pltpu.VMEM(sums, jnp.float32),
        ],
        in_specs=[anywhere] * (2 + len(cell_values)),
        out_specs=[in_vmem, in_vmem],
        scratch_shapes=[
            pltpu.VMEM((chunks, comps, electrodes, LANES), fields.dtype),
            pltpu.VMEM((2, 2 * comps, readings, LANES), jnp.float32),
            pltpu.VMEM((readings, LANES), jnp.float32),
            pltpu.VMEM((11, chunks, LANES), jnp.float32),
            pltpu.VMEM((4, chunks, LANES), jnp.float32),
            pltpu.VMEM(quads.shape, quads.dtype),
            pltpu.VMEM((4, readings, LANES), jnp.bfloat16),
            pltpu.VMEM((4, readings, LANES), jnp.bfloat16),
            pltpu.VMEM(sums, jnp.float32),
            pltpu.VMEM((n, *sums), jnp.float32),
            pltpu.SemaphoreType.DMA((chunks, n)),
            pltpu.SemaphoreType.DMA((chunks, n)),
            pltpu.SemaphoreType.DMA((chunks,)),
            pltpu.SemaphoreType.DMA((5,)),
            pltpu.SemaphoreType.DMA((n,)),
            pltpu.SemaphoreType.DMA((n,)),
        ],
        compiler_params=pltpu.CompilerParams(
            collective_id=0, has_side_effects=True, vmem_limit_bytes=40 * 2**20
        ),
        name="exchange",
    )(quads, fields, *cell_values)


def norm_kernel(count, sens, total, jacobian, coverage, scale, sums_of):
    depth = total.shape[0]
    readings, _, cells = jacobian.shape
    step = pl.program_id(0)

    @pl.when(step == 0)
    def _():
        sums_of[...] = jnp.zeros_like(sums_of)
        value = lax.rsqrt(total[...] / count + 1e-06)
        for p in range(4):
            scale[pl.ds(p, depth, stride=4), :] = value

    wide = 4 * depth
    lane = lax.broadcasted_iota(jnp.int32, (wide, LANES), 1)

    first = step * (readings // depth)

    def some(g, sums):
        columns = [
            jnp.sum(jnp.where(lane == first + UNROLL * g + u, scale[...], 0.0), axis=-1, keepdims=True)
            for u in range(UNROLL)
        ]
        for u in range(UNROLL):
            i = UNROLL * g + u
            rows = pl.ds(pl.multiple_of((first + i) * wide, wide), wide)
            put = pl.ds(pl.multiple_of(i * depth, depth), depth)
            for c in range(cells // LANES):
                normed = sens[c, rows, :] * columns[u]
                jacobian[put, :, pl.ds(c * LANES, LANES)] = normed.reshape(depth, 4, LANES).astype(jnp.bfloat16)
                square = jnp.sum((normed * normed).reshape(wide // 8, 8, LANES), axis=0)
                sums = sums[:c] + (sums[c] + square,) + sums[c + 1:]
        return sums

    sums = lax.fori_loop(
        0, readings // depth // UNROLL, some,
        tuple(sums_of[c] for c in range(cells // LANES)),
    )
    for c, total_of in enumerate(sums):
        sums_of[c] = total_of

    @pl.when(step == pl.num_programs(0) - 1)
    def _():
        for c in range(cells // LANES):
            coverage[pl.ds(c, 1), :] = jnp.sum(sums_of[c], axis=0, keepdims=True)


def normalise(sens, total, count):
    chunks, rows, _ = sens.shape
    readings, cells = rows // 4, chunks * LANES
    block = 512
    return pl.pallas_call(
        functools.partial(norm_kernel, count),
        grid=(readings // block,),
        in_specs=[
            pl.BlockSpec(memory_space=pltpu.VMEM),
            pl.BlockSpec(memory_space=pltpu.VMEM),
        ],
        out_specs=[
            pl.BlockSpec((block, 4, cells), lambda i: (i, 0, 0)),
            pl.BlockSpec((chunks, LANES), lambda i: (0, 0)),
        ],
        out_shape=[
            jax.ShapeDtypeStruct((readings, 4, cells), jnp.bfloat16),
            jax.ShapeDtypeStruct((chunks, LANES), jnp.float32),
        ],
        scratch_shapes=[
            pltpu.VMEM((4 * total.shape[0], LANES), jnp.float32),
            pltpu.VMEM((chunks, 8, LANES), jnp.float32),
        ],
        compiler_params=pltpu.CompilerParams(vmem_limit_bytes=8 * 2**20),
        name="norm",
    )(*(pltpu.with_memory_space_constraint(x, pltpu.VMEM) for x in (sens, total)))


def local(fields, horiz, vertical, tilt_angle, azimuth, electrode_quads):
    shards = lax.axis_size("cell")
    cells = horiz.shape[0]
    sens, total = sensitivities(
        fields.transpose(1, 0, 2),
        electrode_quads.T,
        [x.reshape(cells // LANES, LANES) for x in (horiz, vertical, tilt_angle, azimuth)],
        shards,
    )
    jacobian, coverage = normalise(sens, total, 4.0 * cells * shards)
    return jacobian, coverage.reshape(-1)


def solution(mesh):
    placed = (
        P(("grp", "cell"), None, None),
        P(("grp", "cell")),
        P(("grp", "cell")),
        P(("grp", "cell")),
        P(("grp", "cell")),
        P("grp", None),
    )
    return jax.shard_map(
        local,
        mesh=mesh,
        in_specs=placed,
        out_specs=(P("grp", None, "cell"), P(("grp", "cell"))),
        check_vma=False,
    )
```

```python
import functools

import jax
import jax.numpy as jnp
from jax import lax
from jax.experimental import pallas as pl
from jax.experimental.pallas import tpu as pltpu
from jax.sharding import PartitionSpec as P

MESH = pl.DeviceIdType.MESH
LANES = 128
DEPTH = 256
PARTS = 8
SLOTS = 4
UNROLL = 16
TILE = 1024


def greet(n, me):
    barrier = pltpu.get_barrier_semaphore()

    @pl.loop(1, n)
    def _(step):
        pl.semaphore_signal(barrier, inc=1, device_id={"cell": lax.rem(me + step, n)}, device_id_type=MESH)

    pl.semaphore_wait(barrier, n - 1)


def fill_coefficients(coef, horiz, vertical, tilt_angle, azimuth):
    sin_t, cos_t = jnp.sin(tilt_angle), jnp.cos(tilt_angle)
    sin_p, cos_p = jnp.sin(azimuth), jnp.cos(azimuth)
    rows = (
        sin_t * cos_p, sin_t * sin_p, cos_t,
        cos_t * cos_p, cos_t * sin_p, -sin_t,
        -sin_t * sin_p, sin_t * cos_p,
        -horiz, -vertical, horiz - vertical,
    )
    for k, row in enumerate(rows):
        coef[k] = row


def spread_quads(quads, block_of, place_of):
    for k in range(4):
        @pl.loop(0, quads.shape[1] // LANES)
        def _(i):
            at = pl.multiple_of(i * LANES, LANES)
            row = quads[pl.ds(k, 1), pl.ds(at, LANES)]
            block = row // DEPTH
            for target, value in ((block_of, block), (place_of, row - block * DEPTH)):
                wide = jnp.broadcast_to(value.astype(jnp.float32), (LANES, LANES))
                target[k, pl.ds(at, LANES), :] = wide.T.astype(jnp.bfloat16)


def add_group(chunk, group, landed, block_of, place_of, diffs):
    readings = diffs.shape[2]
    lane = lax.broadcasted_iota(jnp.int32, (TILE, LANES), 1).astype(jnp.float32)
    lanes = [(lane + LANES * h).astype(jnp.bfloat16) for h in range(DEPTH // LANES)]
    here = jnp.full((TILE, LANES), group, jnp.int32).astype(jnp.float32).astype(jnp.bfloat16)
    one, none = jnp.bfloat16(1), jnp.bfloat16(0)
    away = jnp.bfloat16(-1)

    @pl.loop(0, readings // TILE)
    def _(t):
        at = pl.multiple_of(t * TILE, TILE)
        rows = pl.ds(pl.multiple_of(group * DEPTH, DEPTH), DEPTH)
        grads = jnp.concatenate([landed[chunk, c, rows, :] for c in range(3)], axis=-1)
        for pair in range(2):
            plus, minus = (
                jnp.where(block_of[k, pl.ds(at, TILE), :] == here, place_of[k, pl.ds(at, TILE), :], away)
                for k in (2 * pair, 2 * pair + 1)
            )
            select = jnp.concatenate(
                [jnp.where(plus == x, one, jnp.where(minus == x, -one, none)) for x in lanes], axis=-1
            )
            out = jnp.dot(select, grads, preferred_element_type=jnp.float32)
            for c in range(3):
                diffs[chunk % 2, 3 * pair + c, pl.ds(at, TILE), :] += out[:, c * LANES:(c + 1) * LANES]


def chunk_sensitivities(chunk, coef, diffs, sens, squares):
    readings = squares.shape[0]
    tile = 32

    @pl.loop(0, readings // tile)
    def _(i):
        at = pl.multiple_of(i * tile, tile)
        s = [diffs[chunk % 2, c, pl.ds(at, tile), :] for c in range(3)]
        r = [diffs[chunk % 2, 3 + c, pl.ds(at, tile), :] for c in range(3)]
        k = [coef[j, pl.ds(chunk, 1), :] for j in range(11)]
        sn, rn = (f[0] * k[0] + f[1] * k[1] + f[2] * k[2] for f in (s, r))
        st, rt = (f[0] * k[3] + f[1] * k[4] + f[2] * k[5] for f in (s, r))
        sp, rp = (f[0] * k[6] + f[1] * k[7] for f in (s, r))
        dot = s[0] * r[0] + s[1] * r[1] + s[2] * r[2]
        both = sn * rn
        values = (
            k[8] * (dot - both), k[9] * both, k[10] * (st * rn + sn * rt), k[10] * (sp * rn + sn * rp)
        )
        square = squares[pl.ds(at, tile), :]
        for p, value in enumerate(values):
            sens[chunk, pl.ds(4 * at + p, tile, stride=4), :] = value
            square = square + value * value
        squares[pl.ds(at, tile), :] = square


def flip(a, b, n):
    out, weight = 0, 1
    while weight < n:
        out = out + (a // weight + b // weight) % 2 * weight
        weight *= 2
    return out


def exchange_kernel(
    n, quads_hbm, fields, horiz, vertical, tilt_angle, azimuth, sens, total,
    landed, diffs, squares, coef, cells_of, quads, block_of, place_of, part, slots,
    send_sem, recv_sem, own_sem, small_sem, part_sem,
):
    me = lax.axis_index("cell")
    rows = fields.shape[1]
    chunks = landed.shape[0]
    readings = squares.shape[0]
    cells = chunks * LANES
    groups = rows * n // DEPTH
    members = DEPTH // rows
    my_group = me // members
    paired = n & (n - 1) == 0
    greet(n, me)

    def landing(chunk):
        return landed.at[chunk, :, pl.ds(pl.multiple_of(me * rows, rows), rows), :]

    def leaving(device, chunk):
        return fields.at[:, :, pl.ds(pl.multiple_of(device * cells + chunk * LANES, LANES), LANES)]

    def copy(chunk, peer, source):
        return pltpu.make_async_remote_copy(
            src_ref=leaving(peer, chunk),
            dst_ref=landing(chunk),
            send_sem=send_sem.at[chunk],
            recv_sem=recv_sem.at[chunk, source],
            device_id={"cell": peer},
            device_id_type=MESH,
        )

    def own(chunk):
        return pltpu.make_async_copy(leaving(me, chunk), landing(chunk), own_sem.at[chunk])

    def partner(chunk, step):
        around = lax.rem(me + step, n)
        if not paired:
            return around
        last = (chunk + 1) // chunks
        across = flip(me, step % 2 * (n // 2) + step // 2, n)
        return last * across + (1 - last) * around

    half = groups // 2
    upper = my_group // max(half, 1)

    def turn_group(chunk, turn):
        if not paired:
            return lax.rem(my_group - turn + groups, groups)
        across = flip(my_group, turn, groups)
        far = turn // half
        last = (chunk + 1) // chunks
        inward = upper * (turn - half) + (1 - upper) * (groups - 1 - (turn - half))
        direct = far * (1 - last)
        return direct * inward + (1 - direct) * across

    @pl.loop(0, chunks)
    def _(chunk):
        @pl.loop(1, n)
        def _(step):
            copy(chunk, partner(chunk, step), me).start()

        own(chunk).start()

    smalls = [pltpu.make_async_copy(quads_hbm, quads, small_sem.at[4])] + [
        pltpu.make_async_copy(x, cells_of.at[k], small_sem.at[k])
        for k, x in enumerate((horiz, vertical, tilt_angle, azimuth))
    ]
    for small in smalls:
        small.start()
    squares[...] = jnp.zeros_like(squares)
    for small in smalls:
        small.wait()
    fill_coefficients(coef, *(cells_of[k] for k in range(4)))
    spread_quads(quads, block_of, place_of)

    def take(chunk, first, count):
        @pl.loop(0, count)
        def _(turn):
            group = turn_group(chunk, first + turn)

            @pl.loop(0, members)
            def _(k):
                source = group * members + k

                @pl.when(source == me)
                def _():
                    own(chunk).wait()

                @pl.when(source != me)
                def _():
                    copy(chunk, source, source).wait_recv()

            add_group(chunk, group, landed, block_of, place_of, diffs)

    def take_near(chunk):
        @pl.loop(0, readings // LANES)
        def _(i):
            at = pl.multiple_of(i * LANES, LANES)
            for c in range(6):
                diffs[chunk % 2, c, pl.ds(at, LANES), :] = jnp.zeros((LANES, LANES), jnp.float32)

        take(chunk, 0, half)

    take_near(0)

    @pl.loop(0, chunks)
    def _(chunk):
        @pl.when(chunk + 1 < chunks)
        def _():
            take_near(chunk + 1)

        take(chunk, half, groups - half)
        chunk_sensitivities(chunk, coef, diffs, sens, squares)

    def copy_part(step):
        peer = flip(me, n - step, n) if paired else lax.rem(me + n - step, n)
        return pltpu.make_async_remote_copy(
            src_ref=part,
            dst_ref=slots.at[step],
            send_sem=part_sem.at[0],
            recv_sem=part_sem.at[1],
            device_id={"cell": peer},
            device_id_type=MESH,
        )

    depth = readings // LANES
    lane = lax.broadcasted_iota(jnp.int32, (depth, LANES), 1)

    def gather_sum(j, packed):
        at = pl.multiple_of(j * depth, depth)
        return jnp.where(lane == j, jnp.sum(squares[pl.ds(at, depth), :], axis=-1, keepdims=True), packed)

    part[...] = lax.fori_loop(0, LANES, gather_sum, jnp.zeros((depth, LANES), jnp.float32), unroll=32)

    @pl.loop(1, n)
    def _(step):
        copy_part(step).start()

    slots[0] = part[...]

    def wait_bytes(ref, sem):
        pltpu.make_async_copy(ref, ref, sem).wait()

    @pl.loop(0, chunks)
    def _(chunk):
        wait_bytes(landed.at[chunk, :, pl.ds(0, rows * (n - 1)), :], send_sem.at[chunk])

    for k in range(2):
        wait_bytes(slots.at[pl.ds(1, n - 1)], part_sem.at[k])

    total[...] = jnp.sum(slots[...], axis=0)


def sensitivities(fields, quads, cell_values, n):
    comps, rows, _ = fields.shape
    chunks = cell_values[0].shape[0]
    electrodes, readings = rows * n, quads.shape[1]
    sums = (readings // LANES, LANES)
    in_vmem = pl.BlockSpec(memory_space=pltpu.VMEM)
    anywhere = pl.BlockSpec(memory_space=pl.ANY)
    return pl.pallas_call(
        functools.partial(exchange_kernel, n),
        out_shape=[
            pltpu.VMEM((chunks, readings * 4, LANES), jnp.float32),
            pltpu.VMEM(sums, jnp.float32),
        ],
        in_specs=[anywhere] * (2 + len(cell_values)),
        out_specs=[in_vmem, in_vmem],
        scratch_shapes=[
            pltpu.VMEM((chunks, comps, electrodes, LANES), fields.dtype),
            pltpu.VMEM((2, 2 * comps, readings, LANES), jnp.float32),
            pltpu.VMEM((readings, LANES), jnp.float32),
            pltpu.VMEM((11, chunks, LANES), jnp.float32),
            pltpu.VMEM((4, chunks, LANES), jnp.float32),
            pltpu.VMEM(quads.shape, quads.dtype),
            pltpu.VMEM((4, readings, LANES), jnp.bfloat16),
            pltpu.VMEM((4, readings, LANES), jnp.bfloat16),
            pltpu.VMEM(sums, jnp.float32),
            pltpu.VMEM((n, *sums), jnp.float32),
            pltpu.SemaphoreType.DMA((chunks,)),
            pltpu.SemaphoreType.DMA((chunks, n)),
            pltpu.SemaphoreType.DMA((chunks,)),
            pltpu.SemaphoreType.DMA((5,)),
            pltpu.SemaphoreType.DMA((2,)),
        ],
        compiler_params=pltpu.CompilerParams(
            collective_id=0, has_side_effects=True, vmem_limit_bytes=40 * 2**20
        ),
        name="exchange",
    )(quads, fields, *cell_values)


def norm_kernel(count, sens, total, jacobian, coverage, scale, staged, out_sem):
    depth = total.shape[0]
    readings, _, cells = jacobian.shape
    slots, piece = staged.shape[:2]
    unroll = piece // depth
    wide = 4 * depth
    value = lax.rsqrt(total[...] / count + 1e-06)
    for p in range(4):
        scale[pl.ds(p, depth, stride=4), :] = value
    lane = lax.broadcasted_iota(jnp.int32, (wide, LANES), 1)

    def out(g):
        to = jacobian.at[pl.ds(pl.multiple_of(g * piece, piece), piece)]
        return pltpu.make_async_copy(staged.at[g % slots], to, out_sem.at[g % slots])

    def some(g, sums):
        @pl.when(g >= slots)
        def _():
            out(g - slots).wait()

        columns = [
            jnp.sum(jnp.where(lane == unroll * g + u, scale[...], 0.0), axis=-1, keepdims=True)
            for u in range(unroll)
        ]
        for u in range(unroll):
            rows = pl.ds(pl.multiple_of((unroll * g + u) * wide, wide), wide)
            for c in range(cells // LANES):
                normed = sens[c, rows, :] * columns[u]
                staged[g % slots, pl.ds(u * depth, depth), :, pl.ds(c * LANES, LANES)] = normed.reshape(
                    depth, 4, LANES
                ).astype(jnp.bfloat16)
                square = jnp.sum((normed * normed).reshape(wide // 8, 8, LANES), axis=0)
                sums = sums[:c] + (sums[c] + square,) + sums[c + 1:]
        part = piece // PARTS
        for h in range(PARTS):
            pltpu.make_async_copy(
                staged.at[g % slots, pl.ds(h * part, part)],
                jacobian.at[pl.ds(pl.multiple_of(g * piece + h * part, part), part)],
                out_sem.at[g % slots],
            ).start()
        return sums

    pieces = readings // piece
    sums = lax.fori_loop(0, pieces, some, (jnp.zeros((8, LANES), jnp.float32),) * (cells // LANES))
    for c, sum_of in enumerate(sums):
        coverage[pl.ds(c, 1), :] = jnp.sum(sum_of, axis=0, keepdims=True)

    @pl.loop(max(pieces - slots, 0), pieces)
    def _(g):
        out(g).wait()


def normalise(sens, total, count):
    chunks, rows, _ = sens.shape
    readings, cells = rows // 4, chunks * LANES
    piece = UNROLL * total.shape[0]
    slots = min(SLOTS, readings // piece)
    in_vmem = pl.BlockSpec(memory_space=pltpu.VMEM)
    return pl.pallas_call(
        functools.partial(norm_kernel, count),
        in_specs=[in_vmem, in_vmem],
        out_specs=[pl.BlockSpec(memory_space=pl.ANY), in_vmem],
        out_shape=[
            jax.ShapeDtypeStruct((readings, 4, cells), jnp.bfloat16),
            jax.ShapeDtypeStruct((chunks, LANES), jnp.float32),
        ],
        scratch_shapes=[
            pltpu.VMEM((4 * total.shape[0], LANES), jnp.float32),
            pltpu.VMEM((slots, piece, 4, cells), jnp.bfloat16),
            pltpu.SemaphoreType.DMA((slots,)),
        ],
        compiler_params=pltpu.CompilerParams(vmem_limit_bytes=8 * 2**20),
        name="norm",
    )(*(pltpu.with_memory_space_constraint(x, pltpu.VMEM) for x in (sens, total)))


def local(fields, horiz, vertical, tilt_angle, azimuth, electrode_quads):
    shards = lax.axis_size("cell")
    cells = horiz.shape[0]
    sens, total = sensitivities(
        fields.transpose(1, 0, 2),
        electrode_quads.T,
        [x.reshape(cells // LANES, LANES) for x in (horiz, vertical, tilt_angle, azimuth)],
        shards,
    )
    jacobian, coverage = normalise(sens, total, 4.0 * cells * shards)
    return jacobian, coverage.reshape(-1)


def solution(mesh):
    placed = (
        P(("grp", "cell"), None, None),
        P(("grp", "cell")),
        P(("grp", "cell")),
        P(("grp", "cell")),
        P(("grp", "cell")),
        P("grp", None),
    )
    return jax.shard_map(
        local,
        mesh=mesh,
        in_specs=placed,
        out_specs=(P("grp", None, "cell"), P(("grp", "cell"))),
        check_vma=False,
    )
```

```python
import functools

import jax
import jax.numpy as jnp
from jax import lax
from jax.experimental import pallas as pl
from jax.experimental.pallas import tpu as pltpu
from jax.sharding import PartitionSpec as P

MESH = pl.DeviceIdType.MESH
LANES = 128
DEPTH = 256
PARTS = 8
SLOTS = 4
UNROLL = 16
TILE = 2048


def greet(n, me):
    barrier = pltpu.get_barrier_semaphore()

    @pl.loop(1, n)
    def _(step):
        pl.semaphore_signal(barrier, inc=1, device_id={"cell": lax.rem(me + step, n)}, device_id_type=MESH)

    pl.semaphore_wait(barrier, n - 1)


def fill_coefficients(coef, horiz, vertical, tilt_angle, azimuth):
    sin_t, cos_t = jnp.sin(tilt_angle), jnp.cos(tilt_angle)
    sin_p, cos_p = jnp.sin(azimuth), jnp.cos(azimuth)
    rows = (
        sin_t * cos_p, sin_t * sin_p, cos_t,
        cos_t * cos_p, cos_t * sin_p, -sin_t,
        -sin_t * sin_p, sin_t * cos_p,
        -horiz, -vertical, horiz - vertical,
    )
    for k, row in enumerate(rows):
        coef[k] = row


def spread_quads(quads, block_of, place_of):
    for k in range(4):
        @pl.loop(0, quads.shape[1] // LANES)
        def _(i):
            at = pl.multiple_of(i * LANES, LANES)
            row = quads[pl.ds(k, 1), pl.ds(at, LANES)]
            block = row // DEPTH
            for target, value in ((block_of, block), (place_of, row - block * DEPTH)):
                wide = jnp.broadcast_to(value.astype(jnp.float32), (LANES, LANES))
                target[k, pl.ds(at, LANES), :] = wide.T.astype(jnp.bfloat16)


def add_group(chunk, group, landed, block_of, place_of, diffs):
    readings = diffs.shape[2]
    lane = lax.broadcasted_iota(jnp.int32, (TILE, LANES), 1).astype(jnp.float32)
    lanes = [(lane + LANES * h).astype(jnp.bfloat16) for h in range(DEPTH // LANES)]
    here = jnp.full((TILE, LANES), group, jnp.int32).astype(jnp.float32).astype(jnp.bfloat16)
    one, none = jnp.bfloat16(1), jnp.bfloat16(0)
    away = jnp.bfloat16(-1)

    @pl.loop(0, readings // TILE)
    def _(t):
        at = pl.multiple_of(t * TILE, TILE)
        rows = pl.ds(pl.multiple_of(group * DEPTH, DEPTH), DEPTH)
        grads = jnp.concatenate([landed[chunk, c, rows, :] for c in range(3)], axis=-1)
        for pair in range(2):
            plus, minus = (
                jnp.where(block_of[k, pl.ds(at, TILE), :] == here, place_of[k, pl.ds(at, TILE), :], away)
                for k in (2 * pair, 2 * pair + 1)
            )
            select = jnp.concatenate(
                [jnp.where(plus == x, one, jnp.where(minus == x, -one, none)) for x in lanes], axis=-1
            )
            out = jnp.dot(select, grads, preferred_element_type=jnp.float32)
            for c in range(3):
                diffs[chunk % 2, 3 * pair + c, pl.ds(at, TILE), :] += out[:, c * LANES:(c + 1) * LANES]


def chunk_sensitivities(chunk, coef, diffs, sens, squares):
    readings = squares.shape[0]
    tile = 32

    @pl.loop(0, readings // tile)
    def _(i):
        at = pl.multiple_of(i * tile, tile)
        s = [diffs[chunk % 2, c, pl.ds(at, tile), :] for c in range(3)]
        r = [diffs[chunk % 2, 3 + c, pl.ds(at, tile), :] for c in range(3)]
        k = [coef[j, pl.ds(chunk, 1), :] for j in range(11)]
        sn, rn = (f[0] * k[0] + f[1] * k[1] + f[2] * k[2] for f in (s, r))
        st, rt = (f[0] * k[3] + f[1] * k[4] + f[2] * k[5] for f in (s, r))
        sp, rp = (f[0] * k[6] + f[1] * k[7] for f in (s, r))
        dot = s[0] * r[0] + s[1] * r[1] + s[2] * r[2]
        both = sn * rn
        values = (
            k[8] * (dot - both), k[9] * both, k[10] * (st * rn + sn * rt), k[10] * (sp * rn + sn * rp)
        )
        square = squares[pl.ds(at, tile), :]
        for p, value in enumerate(values):
            sens[chunk, pl.ds(4 * at + p, tile, stride=4), :] = value
            square = square + value * value
        squares[pl.ds(at, tile), :] = square


def flip(a, b, n):
    out, weight = 0, 1
    while weight < n:
        out = out + (a // weight + b // weight) % 2 * weight
        weight *= 2
    return out


def exchange_kernel(
    n, quads_hbm, fields, horiz, vertical, tilt_angle, azimuth, sens, total,
    landed, diffs, squares, coef, cells_of, quads, block_of, place_of, part, slots,
    send_sem, recv_sem, own_sem, small_sem, part_sem,
):
    me = lax.axis_index("cell")
    rows = fields.shape[1]
    chunks = landed.shape[0]
    readings = squares.shape[0]
    cells = chunks * LANES
    groups = rows * n // DEPTH
    members = DEPTH // rows
    my_group = me // members
    paired = n & (n - 1) == 0
    greet(n, me)

    def landing(chunk):
        return landed.at[chunk, :, pl.ds(pl.multiple_of(me * rows, rows), rows), :]

    def leaving(device, chunk):
        return fields.at[:, :, pl.ds(pl.multiple_of(device * cells + chunk * LANES, LANES), LANES)]

    def copy(chunk, peer, source):
        return pltpu.make_async_remote_copy(
            src_ref=leaving(peer, chunk),
            dst_ref=landing(chunk),
            send_sem=send_sem.at[chunk],
            recv_sem=recv_sem.at[chunk, source],
            device_id={"cell": peer},
            device_id_type=MESH,
        )

    def own(chunk):
        return pltpu.make_async_copy(leaving(me, chunk), landing(chunk), own_sem.at[chunk])

    def partner(chunk, step):
        around = lax.rem(me + step, n)
        if not paired:
            return around
        last = (chunk + 1) // chunks
        across = flip(me, step % 2 * (n // 2) + step // 2, n)
        return last * across + (1 - last) * around

    half = groups // 2
    upper = my_group // max(half, 1)

    def turn_group(chunk, turn):
        if not paired:
            return lax.rem(my_group - turn + groups, groups)
        across = flip(my_group, turn, groups)
        far = turn // half
        last = (chunk + 1) // chunks
        inward = upper * (turn - half) + (1 - upper) * (groups - 1 - (turn - half))
        direct = far * (1 - last)
        return direct * inward + (1 - direct) * across

    @pl.loop(0, chunks)
    def _(chunk):
        @pl.loop(1, n)
        def _(step):
            copy(chunk, partner(chunk, step), me).start()

        own(chunk).start()

    smalls = [pltpu.make_async_copy(quads_hbm, quads, small_sem.at[4])] + [
        pltpu.make_async_copy(x, cells_of.at[k], small_sem.at[k])
        for k, x in enumerate((horiz, vertical, tilt_angle, azimuth))
    ]
    for small in smalls:
        small.start()
    squares[...] = jnp.zeros_like(squares)
    for small in smalls:
        small.wait()
    fill_coefficients(coef, *(cells_of[k] for k in range(4)))
    spread_quads(quads, block_of, place_of)

    def take(chunk, first, count):
        @pl.loop(0, count)
        def _(turn):
            group = turn_group(chunk, first + turn)

            @pl.loop(0, members)
            def _(k):
                source = group * members + k

                @pl.when(source == me)
                def _():
                    own(chunk).wait()

                @pl.when(source != me)
                def _():
                    copy(chunk, source, source).wait_recv()

            add_group(chunk, group, landed, block_of, place_of, diffs)

    def take_near(chunk):
        @pl.loop(0, readings // LANES)
        def _(i):
            at = pl.multiple_of(i * LANES, LANES)
            for c in range(6):
                diffs[chunk % 2, c, pl.ds(at, LANES), :] = jnp.zeros((LANES, LANES), jnp.float32)

        take(chunk, 0, half)

    take_near(0)

    @pl.loop(0, chunks)
    def _(chunk):
        @pl.when(chunk + 1 < chunks)
        def _():
            take_near(chunk + 1)

        take(chunk, half, groups - half)
        chunk_sensitivities(chunk, coef, diffs, sens, squares)

    def copy_part(step):
        peer = flip(me, n - step, n) if paired else lax.rem(me + n - step, n)
        return pltpu.make_async_remote_copy(
            src_ref=part,
            dst_ref=slots.at[step],
            send_sem=part_sem.at[0],
            recv_sem=part_sem.at[1],
            device_id={"cell": peer},
            device_id_type=MESH,
        )

    depth = readings // LANES
    lane = lax.broadcasted_iota(jnp.int32, (depth, LANES), 1)

    def gather_sum(j, packed):
        at = pl.multiple_of(j * depth, depth)
        return jnp.where(lane == j, jnp.sum(squares[pl.ds(at, depth), :], axis=-1, keepdims=True), packed)

    part[...] = lax.fori_loop(0, LANES, gather_sum, jnp.zeros((depth, LANES), jnp.float32), unroll=32)

    @pl.loop(1, n)
    def _(step):
        copy_part(step).start()

    slots[0] = part[...]

    def wait_bytes(ref, sem):
        pltpu.make_async_copy(ref, ref, sem).wait()

    @pl.loop(0, chunks)
    def _(chunk):
        wait_bytes(landed.at[chunk, :, pl.ds(0, rows * (n - 1)), :], send_sem.at[chunk])

    for k in range(2):
        wait_bytes(slots.at[pl.ds(1, n - 1)], part_sem.at[k])

    total[...] = jnp.sum(slots[...], axis=0)


def sensitivities(fields, quads, cell_values, n):
    comps, rows, _ = fields.shape
    chunks = cell_values[0].shape[0]
    electrodes, readings = rows * n, quads.shape[1]
    sums = (readings // LANES, LANES)
    in_vmem = pl.BlockSpec(memory_space=pltpu.VMEM)
    anywhere = pl.BlockSpec(memory_space=pl.ANY)
    return pl.pallas_call(
        functools.partial(exchange_kernel, n),
        out_shape=[
            pltpu.VMEM((chunks, readings * 4, LANES), jnp.float32),
            pltpu.VMEM(sums, jnp.float32),
        ],
        in_specs=[anywhere] * (2 + len(cell_values)),
        out_specs=[in_vmem, in_vmem],
        scratch_shapes=[
            pltpu.VMEM((chunks, comps, electrodes, LANES), fields.dtype),
            pltpu.VMEM((2, 2 * comps, readings, LANES), jnp.float32),
            pltpu.VMEM((readings, LANES), jnp.float32),
            pltpu.VMEM((11, chunks, LANES), jnp.float32),
            pltpu.VMEM((4, chunks, LANES), jnp.float32),
            pltpu.VMEM(quads.shape, quads.dtype),
            pltpu.VMEM((4, readings, LANES), jnp.bfloat16),
            pltpu.VMEM((4, readings, LANES), jnp.bfloat16),
            pltpu.VMEM(sums, jnp.float32),
            pltpu.VMEM((n, *sums), jnp.float32),
            pltpu.SemaphoreType.DMA((chunks,)),
            pltpu.SemaphoreType.DMA((chunks, n)),
            pltpu.SemaphoreType.DMA((chunks,)),
            pltpu.SemaphoreType.DMA((5,)),
            pltpu.SemaphoreType.DMA((2,)),
        ],
        compiler_params=pltpu.CompilerParams(
            collective_id=0, has_side_effects=True, vmem_limit_bytes=40 * 2**20
        ),
        name="exchange",
    )(quads, fields, *cell_values)


def norm_kernel(count, sens, total, jacobian, coverage, scale, staged, out_sem):
    depth = total.shape[0]
    readings, _, cells = jacobian.shape
    slots, piece = staged.shape[:2]
    unroll = piece // depth
    wide = 4 * depth
    value = lax.rsqrt(total[...] / count + 1e-06)
    for p in range(4):
        scale[pl.ds(p, depth, stride=4), :] = value
    lane = lax.broadcasted_iota(jnp.int32, (wide, LANES), 1)

    def out(g):
        to = jacobian.at[pl.ds(pl.multiple_of(g * piece, piece), piece)]
        return pltpu.make_async_copy(staged.at[g % slots], to, out_sem.at[g % slots])

    def some(g, sums):
        @pl.when(g >= slots)
        def _():
            out(g - slots).wait()

        columns = [
            jnp.sum(jnp.where(lane == unroll * g + u, scale[...], 0.0), axis=-1, keepdims=True)
            for u in range(unroll)
        ]
        for u in range(unroll):
            rows = pl.ds(pl.multiple_of((unroll * g + u) * wide, wide), wide)
            for c in range(cells // LANES):
                normed = sens[c, rows, :] * columns[u]
                staged[g % slots, pl.ds(u * depth, depth), :, pl.ds(c * LANES, LANES)] = normed.reshape(
                    depth, 4, LANES
                ).astype(jnp.bfloat16)
                square = jnp.sum((normed * normed).reshape(wide // 8, 8, LANES), axis=0)
                sums = sums[:c] + (sums[c] + square,) + sums[c + 1:]
        part = piece // PARTS
        for h in range(PARTS):
            pltpu.make_async_copy(
                staged.at[g % slots, pl.ds(h * part, part)],
                jacobian.at[pl.ds(pl.multiple_of(g * piece + h * part, part), part)],
                out_sem.at[g % slots],
            ).start()
        return sums

    pieces = readings // piece
    sums = lax.fori_loop(0, pieces, some, (jnp.zeros((8, LANES), jnp.float32),) * (cells // LANES))
    for c, sum_of in enumerate(sums):
        coverage[pl.ds(c, 1), :] = jnp.sum(sum_of, axis=0, keepdims=True)

    @pl.loop(max(pieces - slots, 0), pieces)
    def _(g):
        out(g).wait()


def normalise(sens, total, count):
    chunks, rows, _ = sens.shape
    readings, cells = rows // 4, chunks * LANES
    piece = UNROLL * total.shape[0]
    slots = min(SLOTS, readings // piece)
    in_vmem = pl.BlockSpec(memory_space=pltpu.VMEM)
    return pl.pallas_call(
        functools.partial(norm_kernel, count),
        in_specs=[in_vmem, in_vmem],
        out_specs=[pl.BlockSpec(memory_space=pl.ANY), in_vmem],
        out_shape=[
            jax.ShapeDtypeStruct((readings, 4, cells), jnp.bfloat16),
            jax.ShapeDtypeStruct((chunks, LANES), jnp.float32),
        ],
        scratch_shapes=[
            pltpu.VMEM((4 * total.shape[0], LANES), jnp.float32),
            pltpu.VMEM((slots, piece, 4, cells), jnp.bfloat16),
            pltpu.SemaphoreType.DMA((slots,)),
        ],
        compiler_params=pltpu.CompilerParams(vmem_limit_bytes=8 * 2**20),
        name="norm",
    )(*(pltpu.with_memory_space_constraint(x, pltpu.VMEM) for x in (sens, total)))


def local(fields, horiz, vertical, tilt_angle, azimuth, electrode_quads):
    shards = lax.axis_size("cell")
    cells = horiz.shape[0]
    sens, total = sensitivities(
        fields.transpose(1, 0, 2),
        electrode_quads.T,
        [x.reshape(cells // LANES, LANES) for x in (horiz, vertical, tilt_angle, azimuth)],
        shards,
    )
    jacobian, coverage = normalise(sens, total, 4.0 * cells * shards)
    return jacobian, coverage.reshape(-1)


def solution(mesh):
    placed = (
        P(("grp", "cell"), None, None),
        P(("grp", "cell")),
        P(("grp", "cell")),
        P(("grp", "cell")),
        P(("grp", "cell")),
        P("grp", None),
    )
    return jax.shard_map(
        local,
        mesh=mesh,
        in_specs=placed,
        out_specs=(P("grp", None, "cell"), P(("grp", "cell"))),
        check_vma=False,
    )
```
